32 devices in a mesh: gx: 4 (over z), gy: 4 (over x, core), gz: 2 (over y).
Axes of the slice: x: 2, y: 2, z: 4, core: 2. Of those that a mesh axis runs over, the one named last changes fastest.
Arguments:
- vel: float32 [3, 64, 64, 512], P(None, 'gz', 'gx', 'gy'), may hold values from -6 to 6
- pres: float32 [64, 64, 512], P('gz', 'gx', 'gy'), may hold values from -6 to 6
- modulus: float32 [64, 64, 512], P('gz', 'gx', 'gy'), may hold values from 0.05 to 0.5
- adj_vel_in: float32 [3, 64, 64, 512], P(None, 'gz', 'gx', 'gy'), may hold values from -6 to 6
- adj_pres_in: float32 [64, 64, 512], P('gz', 'gx', 'gy'), may hold values from -6 to 6
- sensor_values: float32 [1024, 128], P(('gx', 'gy', 'gz')), may hold values from -6 to 6
- sensor_owner: int32 [1024, 1], P(('gx', 'gy', 'gz')), may hold values from 0 to 15; in each aligned block of 32 rows (0 to 31, 32 to 63, ...) at most 4 rows name the same one
- sensor_line: int32 [1024], P(('gx', 'gy', 'gz')), may hold values from 0 to 15
- sensor_step: int32 [1024], P(('gx', 'gy', 'gz')), may hold values from 0 to 1
Outputs:
- adj_vel: float32 [3, 64, 64, 512], P(None, 'gz', 'gx', 'gy')
- adj_pres: float32 [64, 64, 512], P('gz', 'gx', 'gy')
- shear_gradient: float32 [64, 64, 512], P('gz', 'gx', 'gy')
The draws below stay inside these ranges and needn't reach their ends.
Inputs may be any that keep to these rules, and one draw needn't show every extreme that they name: `sensor_owner`: among the 32 rows of one device at most 4 name the same surface brick, and in every draw some device has 4 rows for one brick.
All inputs are finite; a program needn't handle non-finite values.
Results may differ from the reference program's by a relative error of at most 0.00011.
Values sent between devices are 32-bit elements; how exact they have to be, the bound alone decides.
No kernel may reach another device: no remote copies, remote signals or barrier semaphores. Data moves between devices by JAX's collectives and lax.ppermute only.
A program may use at most 64 MiB of HBM per device.

```python
import math
import jax
import jax.numpy as jnp
import numpy as np
from jax import lax

CX = 16
CY = 128
STEPS = 2
R_DEV = 32
CAP = 4
NX = 64
NY = 512
NZ = 64
ROWS = 1024
N_GX = 4
N_GY = 4


def plant(array, key, least, largest):
    longest = array.shape.index(max(array.shape))
    spots = []
    for shift in (0, 1):
        where = [jax.random.randint(jax.random.fold_in(key, axis), (), 0, length) for axis, length in enumerate(array.shape)]
        where[longest] = (where[longest] + shift) % array.shape[longest]
        spots.append(tuple(where))
    return array.at[spots[0]].set(least).at[spots[1]].set(largest)


def shard_levels(key, shape, split, least, largest):
    loudness = 1.0
    for dim, shards_of in split:
        steps = jax.random.uniform(jax.random.fold_in(jax.random.fold_in(key, 6), dim), (shards_of,), jnp.float32, least / len(split), largest / len(split))
        loudness = loudness * jnp.repeat(jnp.exp(steps), shape[dim] // shards_of).reshape((-1,) + (1,) * (len(shape) - 1 - dim))
    return loudness


def assign_block(key, own, number, rows, amount, top, limit, skew):
    sequence = jax.random.permutation(key, amount)
    heavy_load, ordinary = load_shares(amount, rows * top, limit, skew, True), load_shares(amount, rows * top, limit, skew, False)
    places = jnp.arange(amount)

    def named(lengths, turn):
        used = int((lengths > 0).sum())
        fixed = max(1, used // 4)
        shifted = fixed + (places - fixed + turn * (used - fixed)) % max(1, amount - fixed)
        return jnp.zeros((amount,), jnp.int32).at[sequence[jnp.where(places < fixed, places, shifted)]].set(jnp.asarray(lengths, jnp.int32))

    lengths = jnp.where(number % 4 == 0, named(heavy_load, number // 4), named(ordinary, number - number // 4 - 1))
    mixed = jax.random.permutation(jax.random.fold_in(own, 3), amount)
    donor, sink = mixed[0:amount // 2 * 2:2], mixed[1:amount // 2 * 2:2]
    margin = jnp.minimum(lengths[donor] - 1, limit - lengths[sink]) // 2
    margin = jnp.where((donor == sequence[0]) | (sink == sequence[0]) | (lengths[sink] == 0), 0, jnp.maximum(margin, 0))
    shifted = jax.random.randint(jax.random.fold_in(own, 4), (amount // 2,), 0, 1 << 20) % (margin + 1)
    lengths = lengths.at[donor].add(-shifted).at[sink].add(shifted)
    members = jnp.searchsorted(jnp.cumsum(lengths), jnp.arange(rows * top), side="right").astype(jnp.int32)
    listing = members.reshape(top, rows).T
    listing = listing[jax.random.permutation(jax.random.fold_in(own, 1), rows)]
    turn = jax.random.randint(jax.random.fold_in(own, 2), (rows, 1), 0, top)
    return jnp.take_along_axis(listing, (jnp.arange(top)[None, :] + turn) % top, axis=1)


def load_shares(amount, total, most, lean, full):
    weights = [(1 << 20) // math.isqrt(rank ** lean) + 1 for rank in range(1, amount + 1)]
    largest = most if full else min(most, max(-(-total // amount), total * weights[0] // sum(weights)))
    least = 1 if total - largest >= amount - 1 else 0
    counts, surplus = [largest] + [least] * (amount - 1), total - largest - least * (amount - 1)
    while surplus > 0:
        candidates = [i for i in range(1, amount) if counts[i] < largest] or [i for i in range(1, amount) if counts[i] < most]
        mass, left = sum([weights[i] for i in candidates]), surplus
        for i in candidates:
            extra = min(most - counts[i], max(1, left * weights[i] // mass), surplus)
            counts[i] = counts[i] + extra
            surplus = surplus - extra
    return np.array(counts)


def bell_draw(key, dims, deviation, reach, shards=(), kind=jnp.bfloat16):
    values = jax.random.normal(key, dims, jnp.float32) * deviation
    if len(shards) > 0:
        values = shard_levels(key, dims, shards, -0.22, 0.18) * values
    return jnp.clip(values, min=-reach, max=reach).astype(kind)


def setup_inputs(seed: int = 0) -> dict:
    streams_of = jax.random.split(jax.random.key(seed), 10)
    vel = bell_draw(streams_of[0], (3, NZ, NX, NY), 1.0, 6.0, ((1, 2), (2, 4), (3, 4)), jnp.float32)
    pres = bell_draw(streams_of[1], (NZ, NX, NY), 1.0, 6.0, ((0, 2), (1, 4), (2, 4)), jnp.float32)
    modulus = jnp.clip(jnp.exp(math.log(0.5) - 2.3025851 * jax.random.uniform(streams_of[2], (NZ, NX, NY), jnp.float32) ** shard_levels(streams_of[2], (NZ, NX, NY), ((0, 2), (1, 4), (2, 4)), -0.2, 0.2)), 0.05, 0.5)
    adj_vel_in = bell_draw(streams_of[3], (3, NZ, NX, NY), 1.0, 6.0, ((1, 2), (2, 4), (3, 4)), jnp.float32)
    adj_pres_in = bell_draw(streams_of[4], (NZ, NX, NY), 1.0, 6.0, ((0, 2), (1, 4), (2, 4)), jnp.float32)
    sensor_values = bell_draw(streams_of[5], (ROWS, CY), 1.0, 6.0, ((0, 32),), jnp.float32)
    sensor_owner_keys = jax.random.split(jax.random.fold_in(streams_of[6], 1), ROWS // R_DEV)
    sensor_owner_turns = jax.random.permutation(jax.random.fold_in(streams_of[6], 3), ROWS // R_DEV)
    sensor_owner = jax.vmap(lambda own, number: assign_block(jax.random.fold_in(streams_of[6], 2), own, number, R_DEV, N_GX * N_GY, 1, CAP, 2))(sensor_owner_keys, sensor_owner_turns).reshape((ROWS, 1))
    sensor_line = plant(jax.random.randint(streams_of[7], (ROWS,), 0, CX), jax.random.fold_in(streams_of[7], 1), 0, CX - 1).astype(jnp.int32)
    sensor_step = plant(jax.random.randint(streams_of[8], (ROWS,), 0, STEPS), jax.random.fold_in(streams_of[8], 1), 0, STEPS - 1).astype(jnp.int32)
    return {"vel": vel, "pres": pres, "modulus": modulus, "adj_vel_in": adj_vel_in, "adj_pres_in": adj_pres_in, "sensor_values": sensor_values, "sensor_owner": sensor_owner, "sensor_line": sensor_line, "sensor_step": sensor_step}


def lower(field, axis):
    widths = [(0, 0)] * field.ndim
    widths[axis] = (1, 0)
    return lax.slice_in_dim(jnp.pad(field, widths), 0, field.shape[axis], axis=axis)


def upper(field, axis):
    widths = [(0, 0)] * field.ndim
    widths[axis] = (0, 1)
    return lax.slice_in_dim(jnp.pad(field, widths), 1, field.shape[axis] + 1, axis=axis)


def laplace(field):
    total = upper(field, 0) + lower(field, 0) + upper(field, 1) + lower(field, 1)
    total = total + upper(field, 2) + lower(field, 2)
    return total - 6.0 * field


def divergence(vector):
    along_x = vector[0] - lower(vector[0], 1)
    along_y = vector[1] - lower(vector[1], 2)
    along_z = vector[2] - lower(vector[2], 0)
    return along_x + along_y + along_z


def gradient(field):
    return jnp.stack([upper(field, 1) - field, upper(field, 2) - field, upper(field, 0) - field])


def reference(vel, pres, modulus, adj_vel_in, adj_pres_in, sensor_values, sensor_owner, sensor_line, sensor_step):
    owner = sensor_owner[:, 0]
    xs = (owner // N_GY) * CX + sensor_line
    ys = (owner % N_GY)[:, None] * CY + jnp.arange(CY, dtype=jnp.int32)[None, :]
    forcing = jnp.zeros((STEPS, NX, NY), jnp.float32)
    forcing = forcing.at[sensor_step[:, None], xs[:, None], ys].add(sensor_values)
    state_v, state_p = vel, pres
    saved = []
    for step in range(STEPS):
        bend = jnp.stack([laplace(state_v[c]) for c in range(3)])
        saved.append(bend)
        state_p = state_p + 1.0 * divergence(state_v)
        state_v = state_v + 0.25 * (gradient(state_p) + modulus[None] * bend)
    lam_v, lam_p = adj_vel_in, adj_pres_in
    shear = jnp.zeros(pres.shape, jnp.float32)
    for step in reversed(range(STEPS)):
        lam_v = lam_v.at[2, 0].add(forcing[step])
        shear = shear + 0.25 * jnp.sum(lam_v * saved[step], axis=0)
        middle = lam_p - 0.25 * divergence(lam_v)
        weighted = jnp.stack([laplace(modulus * lam_v[c]) for c in range(3)])
        lam_v = lam_v + 0.25 * weighted - 1.0 * gradient(middle)
        lam_p = middle
    return lam_v, lam_p, shear
```

```python
import functools

import jax
import jax.numpy as jnp
from jax import lax
from jax.experimental import pallas as pl
from jax.experimental.pallas import tpu as pltpu
from jax.sharding import PartitionSpec as P

STEPS = 2
W = 2
COLS = 3 * W
FIELDS = 9
AXES = ("gx", "gy", "gz")


def mate(index, count, second):
    other = index + 1 if (index + second) % 2 == 0 else index - 1
    return other if 0 <= other < count else index


def exchange(value, shape, partner):
    nx, ny, nz = shape
    pairs = []
    for i in range(nx):
        for j in range(ny):
            for k in range(nz):
                a, b, c = partner(i, j, k)
                pairs.append(((i * ny + j) * nz + k, (a * ny + b) * nz + c))
    return lax.ppermute(value, AXES, pairs)


def even(index):
    return lax.rem(index, 2) == 0


VM = pl.BlockSpec(memory_space=pltpu.VMEM)
HBM = pl.BlockSpec(memory_space=pltpu.HBM)
PARAMS = pltpu.CompilerParams(vmem_limit_bytes=40 * 1024 * 1024)


def struct(*shape):
    return jax.ShapeDtypeStruct(shape, jnp.float32)


BASE = 8
EDGE_ROWS = 8 * -(-FIELDS * W * W // 8)


def rows_of(dims):
    cz, cx, _ = dims
    return cz + 2 * W + 1, cx + 2 * BASE, cx + 8


def pack_kernel(vel, pres, mod, av, ap, values, owner, line, step, fields, xa, xb, za, zb, xza, xzb, xzc, xzd, sens, *scratch, dims):
    cz, cx, cy = dims
    own, inputs, sem = scratch[0], scratch[1:4], scratch[4]
    rows = own.shape[0]
    ex, ez = even(lax.axis_index("gx")), even(lax.axis_index("gz"))
    copies = [
        (vel, fields.at[pl.ds(0, 3)]),
        (pres, fields.at[3]),
        (mod, fields.at[4]),
        (av, fields.at[pl.ds(5, 3)]),
        (ap, fields.at[8]),
        (values, own),
        (owner, inputs[0]),
        (line, inputs[1]),
        (step, inputs[2]),
    ]
    copies = [pltpu.make_async_copy(a, b, sem.at[i]) for i, (a, b) in enumerate(copies)]
    for copy in copies:
        copy.start()
    for copy in copies[5:]:
        copy.wait()
    first_row = [inputs[i][...] for i in range(3)]
    code = first_row[0] * (STEPS * cx) + first_row[2] * cx + first_row[1]
    sens[0:rows, :] = own[...]
    sens[rows:rows + 8, :] = jnp.zeros((8, cy), jnp.float32)
    sens[rows:rows + 1, 0:rows] = code.astype(jnp.float32)
    x_rows, z_rows = FIELDS * W * cz, FIELDS * W * cx
    for face, at in ((xa, x_rows), (za, z_rows), (xza, EDGE_ROWS)):
        face[at:at + rows + 8, :] = sens[...]
    for copy in copies[:5]:
        copy.wait()
    for f in range(FIELDS):
        for l in range(W):
            first = fields[f, pl.ds(l, cz, stride=cx), :]
            last = fields[f, pl.ds(cx - W + l, cz, stride=cx), :]
            a = jnp.where(ex, last, first)
            b = jnp.where(ex, first, last)
            xa[pl.ds((f * W + l) * cz, cz), :] = a
            xb[pl.ds((f * W + l) * cz, cz), :] = b
            for x, (near, far) in ((a, (xza, xzc)), (b, (xzb, xzd))):
                near[pl.ds((f * W + l) * W, W), :] = jnp.where(ez, x[cz - W:], x[:W])
                if far is not None:
                    far[pl.ds((f * W + l) * W, W), :] = jnp.where(ez, x[:W], x[cz - W:])
            low = fields[f, pl.ds(l * cx, cx), :]
            high = fields[f, pl.ds((cz - W + l) * cx, cx), :]
            za[pl.ds((f * W + l) * cx, cx), :] = jnp.where(ez, high, low)
            if zb is not None:
                zb[pl.ds((f * W + l) * cx, cx), :] = jnp.where(ez, low, high)


def join_kernel(*refs):
    *ins, out = refs
    rows = out.shape[0] // len(ins)
    for i, ref in enumerate(ins):
        out[i * rows:(i + 1) * rows, :] = ref[ref.shape[0] - rows:, :]


def fill(ext, depths, edges, fields, xs, zs, xzs, dims, place):
    cz, cx, cy = dims
    _, wide, _ = rows_of(dims)
    (ix, nx), _, (iz, nz) = place
    ex, ez = even(ix), even(iz)
    has = {"xl": ix > 0, "xh": ix < nx - 1, "zl": iz > 0, "zh": iz < nz - 1}

    def sides(pair, parity, low, high):
        a, b = pair
        below = jnp.where(parity, 0.0 if b is None else b, a)
        above = jnp.where(parity, a, 0.0 if b is None else b)
        return jnp.where(low, below, 0.0), jnp.where(high, above, 0.0)

    for f in range(FIELDS):
        for plane in range(cz):
            ext[f, pl.ds((plane + W) * wide + BASE, cx), :] = fields[f, pl.ds(plane * cx, cx), :]
        depths[f, pl.ds(W * cx, (8 - 2 * W) * cx), :] = jnp.zeros(((8 - 2 * W) * cx, cy), jnp.float32)
        for l in range(W):
            n = f * W + l
            low, high = sides([x[pl.ds(n * cz, cz), :] for x in xs], ex, has["xl"], has["xh"])
            ext[f, pl.ds(W * wide + BASE + cx + l, cz, stride=wide), :] = high
            ext[f, pl.ds(W * wide + BASE - W + l, cz, stride=wide), :] = low
            low, high = sides([None if z is None else z[pl.ds(n * cx, cx), :] for z in zs], ez, has["zl"], has["zh"])
            ext[f, pl.ds(l * wide + BASE, cx), :] = low
            ext[f, pl.ds((cz + W + l) * wide + BASE, cx), :] = high
            depths[f, pl.ds((8 - W + l) * cx, cx), :] = low
            depths[f, pl.ds(l * cx, cx), :] = high
            got = [None if c is None else c[pl.ds(n * W, W), :] for c in xzs]
            near = sides(got[:2], ex, has["xl"], has["xh"])
            far = sides(got[2:], ex, has["xl"], has["xh"]) if got[2] is not None else (None, None)
            for part, row in ((0, BASE - W + l), (1, BASE + cx + l)):
                low, high = sides((near[part], far[part]), ez, has["zl"], has["zh"])
                edges[f, part * W + l] = jnp.concatenate([high, jnp.zeros((8 - 2 * W, cy), jnp.float32), low])
                for k in range(W):
                    ext[f, pl.ds(k * wide + row, 1), :] = low[k:k + 1]
                    ext[f, pl.ds((cz + W + k) * wide + row, 1), :] = high[k:k + 1]


def lane_of(shape):
    return lax.broadcasted_iota(jnp.int32, shape, 1)


def roll(value, by, axis):
    size = value.shape[axis]
    return pltpu.roll(value, by % size, axis)


def add_strips(low, high, row, x, cy):
    at = COLS * (x + W)
    lane = lane_of(row.shape)
    low = jnp.where(lane >= at + W, roll(row, at + W, 1), low)
    high = jnp.where(lane >= at, roll(row, at - (cy - 2 * W), 1), high)
    return low, high


def strip_kernel(fields, xa, xb, za, zb, xza, xzb, xzc, xzd, ext, strips, ya, yb, depths, edges, *, dims, counts):
    cz, cx, cy = dims
    _, wide, _ = rows_of(dims)
    planes = cz + 8
    place = [(lax.axis_index(a), n) for a, n in zip(AXES, counts)]
    fill(ext, depths, edges, fields, (xa, xb), (za, zb), (xza, xzb, xzc, xzd), dims, place)
    ey = even(place[1][0])
    lane = lane_of((planes, cy))
    middle = (lane % COLS >= W) & (lane % COLS < 2 * W)
    for g in range(FIELDS // 3):
        outs = [jnp.zeros((planes, cy), jnp.float32)] * 2
        for j in range(3):
            f = 3 * g + j
            low = jnp.zeros((planes, cy), jnp.float32)
            high = jnp.zeros((planes, cy), jnp.float32)
            for x in range(-W, cx + W):
                own = ext[f, pl.ds(W * wide + BASE + x, cz, stride=wide), :]
                if 0 <= x < cx:
                    beyond = depths[f, pl.ds(x, 8, stride=cx), :]
                else:
                    beyond = edges[f, x + W if x < 0 else x - cx + W]
                low, high = add_strips(low, high, jnp.concatenate([own, beyond]), x, cy)
            strips[f, 0] = low
            strips[f, 1] = high
            for n, (odd_side, even_side) in enumerate(((low, high), (high, low))):
                mine = jnp.where(middle, jnp.where(ey, even_side, odd_side), 0.0)
                outs[n] = outs[n] + roll(mine, W * (j - 1), 1)
        ya[g] = outs[0]
        yb[g] = outs[1]


def lines_kernel(own_rows, far_rows, ya, yb, *refs, dims, counts, rows, joined):
    _, cx, cy = dims
    nx, ny, _ = counts
    _, _, wide = rows_of(dims)
    outs, dense = refs[:ny], refs[ny]
    ix, iy = lax.axis_index("gx"), lax.axis_index("gy")
    size = rows + 8
    ins = [(ref, i * size) for ref in (own_rows, far_rows) if ref is not None for i in range(ref.shape[0] // size)]
    values = jnp.concatenate([r[at:at + rows, :] for r, at in ins], axis=0)
    code = jnp.concatenate([r[at + rows:at + rows + 1, 0:rows] for r, at in ins], axis=1).astype(jnp.int32)
    owner, rest = code // (STEPS * cx), code % (STEPS * cx)
    step, line = rest // cx, rest % cx
    ox, oy = owner // ny, owner % ny
    row = (ox - ix) * cx + line + W
    key = jnp.where((row >= 0) & (row < cx + 2 * W), (oy * STEPS + step) * wide + row, -1)
    table = lax.broadcasted_iota(jnp.int32, (ny * STEPS * wide, len(ins) * rows), 0) == key
    spread = jnp.dot(
        table.astype(jnp.float32), values, precision=lax.Precision.HIGHEST, preferred_element_type=jnp.float32
    )
    block = STEPS * wide
    dense[0] = jnp.zeros((block, cy), jnp.float32)
    dense[ny + 1] = jnp.zeros((block, cy), jnp.float32)
    for b in range(ny):
        dense[b + 1] = spread[b * block:(b + 1) * block]
    lane = lane_of((1, cy))
    for k in range(ny):
        out, base = outs[k], 0
        if k in joined:
            strip = (ya, yb)[joined.index(k)]
            base = strip.shape[0] * strip.shape[1]
            out[0:base, :] = strip[...].reshape(base, cy)
        at = lax.bitwise_xor(iy, k)
        own, below, above = dense[at + 1], dense[at], dense[at + 2]
        out[base:base + block, :] = own
        out[base + block:base + block + 8, :] = jnp.zeros((8, cy), jnp.float32)
        for s in range(STEPS):
            low = jnp.zeros((1, cy), jnp.float32)
            high = jnp.zeros((1, cy), jnp.float32)
            for x in range(-W, cx + W):
                r = s * wide + x + W
                start = COLS * (x + W)
                low = jnp.where(lane >= start, roll(below[r:r + 1], start - (cy - W), 1), low)
                low, high = add_strips(low, high, own[r:r + 1], x, cy)
                high = jnp.where(lane >= start + 2 * W, roll(above[r:r + 1], start + 2 * W, 1), high)
            out[base + block + 2 * s:base + block + 2 * s + 1, :] = low
            out[base + block + 2 * s + 1:base + block + 2 * s + 2, :] = high


def strip_steps(s, mask, f1, f0):
    v, p, mod, av, ap = s[0:3], s[3], s[4], s[5:8], s[8]

    def keep(a):
        return jnp.where(mask, a, 0.0)

    def lap(a):
        total = roll(a, 1, 0) + roll(a, -1, 0) + roll(a, COLS, 1) + roll(a, -COLS, 1) + roll(a, 1, 1) + roll(a, -1, 1)
        return total - 6.0 * a

    def div(u):
        return (u[0] - roll(u[0], COLS, 1)) + (u[1] - roll(u[1], 1, 1)) + (u[2] - roll(u[2], 1, 0))

    def grad(q):
        return roll(q, -COLS, 1) - q, roll(q, -1, 1) - q, roll(q, -1, 0) - q

    b0 = [lap(a) for a in v]
    g = grad(keep(p + div(v)))
    v1 = [keep(v[c] + 0.25 * (g[c] + mod * b0[c])) for c in range(3)]
    av = [av[0], av[1], av[2] + f1]
    shear = sum(av[c] * lap(v1[c]) for c in range(3))
    m = keep(ap - 0.25 * div(av))
    g = grad(m)
    av = [keep(av[c] + 0.25 * lap(mod * av[c]) - g[c]) for c in range(3)]
    av = [av[0], av[1], av[2] + f0]
    shear = 0.25 * (shear + sum(av[c] * b0[c] for c in range(3)))
    m = keep(m - 0.25 * div(av))
    g = grad(m)
    av = [av[c] + 0.25 * lap(mod * av[c]) - g[c] for c in range(3)]
    return av + [m, shear]


def main_steps(ext, forced_z, force, outs, scratch, dims, place):
    cz, cx, cy = dims
    _, wide, short = rows_of(dims)
    (ix, nx), _, (iz, nz) = place
    out_v, out_p, out_s = outs
    w0, b0, v1, a1, w1, q1 = scratch

    row = lax.broadcasted_iota(jnp.int32, (short, cy), 0)
    inside1 = ((row > 0) & (row <= cx)) | ((row > cx) & (ix < nx - 1)) | ((row == 0) & (ix > 0))
    inside0 = (row < cx) | (ix < nx - 1)

    def keep(a, inside, plane):
        at = iz * cz + plane - W
        return jnp.where(inside & ((at >= 0) & (at < nz * cz)), a, 0.0)

    def lap(below, a, above, lower, upper):
        return (above + below) + (lower + upper) + (roll(a, 1, 1) + roll(a, -1, 1)) - 6.0 * a

    def wider(f, plane, dx=0):
        at = pl.ds(plane * wide + (BASE - 1 + dx), short)
        return forced_z[at, :] if f == 7 else ext[f, at, :]

    def weight(c, plane, dx=0):
        return w0[c, pl.ds(plane * wide + (BASE - 1 + dx), short), :]

    def weigh(plane):
        at = pl.ds(pl.multiple_of(plane * wide, 8), wide)
        for c in range(3):
            w0[c, at, :] = ext[4, at, :] * (forced_z[at, :] if c == 2 else ext[5 + c, at, :])

    def pressure(plane, base, q, scale):
        vx, vy, vz = (wider(base + c, plane) for c in range(3))
        d = (vx - wider(base, plane, -1)) + (vy - roll(vy, 1, 1)) + (vz - wider(base + 2, plane - 1))
        return keep(wider(q, plane) + scale * d, inside1, plane)

    def whole(plane):
        return pl.ds(pl.multiple_of(plane * short, 8), short)

    def first(plane, carry):
        p1, m = carry
        p1_above = pressure(plane + 1, 0, 3, 1.0)
        m_above = pressure(plane + 1, 5, 8, -0.25)
        q1[0, whole(plane + 1), :] = p1_above
        q1[1, whole(plane + 1), :] = m_above
        next_row = pl.ds(plane * short + 1, short)
        g = (q1[0, next_row, :] - p1, roll(p1, -1, 1) - p1, p1_above - p1)
        h = (q1[1, next_row, :] - m, roll(m, -1, 1) - m, m_above - m)
        mod = wider(4, plane)
        weigh(plane + 2)
        for c in range(3):
            v = wider(c, plane)
            bend = lap(wider(c, plane - 1), v, wider(c, plane + 1), wider(c, plane, -1), wider(c, plane, 1))
            b0[c, whole(plane), :] = bend
            v1[c, whole(plane), :] = keep(v + 0.25 * (g[c] + mod * bend), inside1, plane)
            a = wider(5 + c, plane)
            spring = lap(weight(c, plane - 1), weight(c, plane), weight(c, plane + 1), weight(c, plane, -1), weight(c, plane, 1))
            a = keep(a + 0.25 * spring - h[c], inside1, plane)
            if c == 2:
                a = a + jnp.where(plane == W, force[pl.ds(1, short), :], 0.0)
            a1[c, whole(plane), :] = a
            w1[c, whole(plane), :] = mod * a
        return p1_above, m_above

    for plane in range(3):
        weigh(plane)
    begin = (pressure(1, 0, 3, 1.0), pressure(1, 5, 8, -0.25))
    for i in range(2):
        q1[i, whole(1), :] = begin[i]
    lax.fori_loop(1, cz + W + 1, first, begin, unroll=2)

    def step(ref, c, plane, dx=0, count=cx):
        return ref[c, pl.ds(plane * short + (1 + dx), count), :]

    def pressure1(plane):
        ax, ay, az = (step(a1, c, plane, 0, short) for c in range(3))
        d = (ax - step(a1, 0, plane, -1, short)) + (ay - roll(ay, 1, 1)) + (az - step(a1, 2, plane - 1, 0, short))
        return keep(step(q1, 1, plane, 0, short) - 0.25 * d, inside0, plane)

    def second(plane, m):
        m_above = pressure1(plane + 1)
        q1[2, whole(plane + 1), :] = m_above
        m, above = m[:cx], m_above[:cx]
        h = (q1[2, pl.ds(plane * short + 1, cx), :] - m, roll(m, -1, 1) - m, above - m)
        own = pl.ds(pl.multiple_of((plane - W) * cx, 8), cx)
        shear = jnp.zeros((cx, cy), jnp.float32)
        for c in range(3):
            a = step(a1, c, plane)
            bend = lap(
                step(v1, c, plane - 1), step(v1, c, plane), step(v1, c, plane + 1), step(v1, c, plane, -1),
                step(v1, c, plane, 1),
            )
            spring = lap(
                step(w1, c, plane - 1), step(w1, c, plane), step(w1, c, plane + 1), step(w1, c, plane, -1),
                step(w1, c, plane, 1),
            )
            at = pl.ds(pl.multiple_of(plane * wide + BASE, 8), cx)
            at_first = forced_z[at, :] if c == 2 else ext[5 + c, at, :]
            shear = shear + (at_first * bend + a * step(b0, c, plane))
            out_v[c, own, :] = a + 0.25 * spring - h[c]
        out_p[own, :] = m
        out_s[own, :] = 0.25 * shear
        return m_above

    begin = pressure1(W)
    q1[2, whole(W), :] = begin
    lax.fori_loop(W, cz + W, second, begin, unroll=2)


def steps_kernel(ext, strips, *rest, dims, counts, lines, joined):
    cz, cx, cy = dims
    _, wide, short = rows_of(dims)
    planes = cz + 8
    forced = rest[:lines]
    out_v, out_p, out_s, force, forced_z, *scratch = rest[lines:]
    place = [(lax.axis_index(a), n) for a, n in zip(AXES, counts)]
    (ix, nx), (iy, ny), (iz, nz) = place
    block = STEPS * short
    size = block + 8
    total = forced[0][forced[0].shape[0] - size:, :]
    for ref in forced[1:]:
        total = total + ref[ref.shape[0] - size:, :]
    force[...] = jnp.where(iz == 0, total, 0.0)
    surface = pl.ds(W * wide + BASE - W, short)
    forced_z[...] = ext[7]
    forced_z[surface, :] = forced_z[surface, :] + force[pl.ds(short, short), :]
    main_steps(ext, forced_z, force, (out_v, out_p, out_s), scratch, dims, place)

    lane = lane_of((planes, cy))
    depth = lax.broadcasted_iota(jnp.int32, (planes, cy), 0)
    x, col = lane // COLS - W, lane % COLS
    z = jnp.where(depth < cz + W, depth, depth - planes)
    gx, gz = ix * cx + x, iz * cz + z
    solid = (x < cx + W) & (gx >= 0) & (gx < nx * cx) & (gz >= 0) & (gz < nz * cz)
    ey = even(iy)
    yfrom = [forced[k] for k in joined]
    results = []
    for side in range(2):
        s = []
        for f in range(FIELDS):
            g, j = f // 3, f % 3
            a, b = (ref[pl.ds(g * planes, planes), :] for ref in yfrom)
            if side == 0:
                fresh = jnp.where(iy > 0, roll(jnp.where(ey, b, a), -W * j, 1), 0.0)
                s.append(jnp.where(col < W, fresh, strips[f, 0]))
            else:
                fresh = jnp.where(iy < ny - 1, roll(jnp.where(ey, a, b), 2 * W - W * j, 1), 0.0)
                s.append(jnp.where(col >= 2 * W, fresh, strips[f, 1]))
        beyond = (col >= W) | (iy > 0) if side == 0 else (col < 2 * W) | (iy < ny - 1)
        top = depth == 0
        push = [jnp.where(top, force[pl.ds(block + 2 * t + side, 1), :], 0.0) for t in range(STEPS)]
        results.append(strip_steps(s, solid & beyond, push[1], push[0]))
    outs = [out_v.at[0], out_v.at[1], out_v.at[2], out_p, out_s]
    lane = lane_of((cz, cy))
    for low, high, ref in zip(*results, outs):
        low, high = low[:cz], high[:cz]
        for x0 in range(cx):
            start = COLS * (x0 + W)
            value = ref[pl.ds(x0, cz, stride=cx), :]
            value = jnp.where(lane < W, roll(low, -(start + W), 1), value)
            value = jnp.where(lane >= cy - W, roll(high, cy - W - (start + W), 1), value)
            ref[pl.ds(x0, cz, stride=cx), :] = value


def shards(vel, pres, modulus, adj_vel_in, adj_pres_in, sensor_values, sensor_owner, sensor_line, sensor_step):
    counts = tuple(lax.axis_size(a) for a in AXES)
    nx, ny, nz = counts
    dims = pres.shape
    cz, cx, cy = dims
    rows = sensor_values.shape[0]
    size = rows + 8
    planes, wide, short = rows_of(dims)
    deep = nz > 2

    x_rows, z_rows, edge_rows = FIELDS * W * cz, FIELDS * W * cx, EDGE_ROWS
    faces = [x_rows + size, x_rows, z_rows + size, z_rows if deep else None]
    faces += [edge_rows + size, edge_rows, edge_rows if deep else None, edge_rows if deep else None]
    spots = [i for i, n in enumerate(faces) if n is not None]

    def spread_out(refs):
        full = [None] * 8
        for i, ref in zip(spots, refs):
            full[i] = ref
        return full

    def pack(*refs):
        count = 10 + len(spots)
        pack_kernel(*refs[:10], *spread_out(refs[10:count]), *refs[count:], dims=dims)

    small = pltpu.VMEM((1, rows), jnp.int32)
    inputs = [
        vel.reshape(3, cz * cx, cy), pres.reshape(cz * cx, cy), modulus.reshape(cz * cx, cy),
        adj_vel_in.reshape(3, cz * cx, cy), adj_pres_in.reshape(cz * cx, cy), sensor_values,
        sensor_owner.reshape(1, rows), sensor_line.reshape(1, rows), sensor_step.reshape(1, rows),
    ]
    fields, *packed, sens = pl.pallas_call(
        pack, out_shape=[pltpu.VMEM((FIELDS, cz * cx, cy), jnp.float32)] + [struct(faces[i], cy) for i in spots] + [struct(size, cy)],
        in_specs=[HBM] * 9, out_specs=[VM] * (len(spots) + 2),
        scratch_shapes=[pltpu.VMEM((rows, cy), jnp.float32), small, small, small, pltpu.SemaphoreType.DMA((9,))],
        compiler_params=PARAMS, name="pack",
    )(*[pltpu.with_memory_space_constraint(x, pltpu.HBM) for x in inputs])
    seconds = [(0, None), (1, None), (None, 0), (None, 1), (0, 0), (1, 0), (0, 1), (1, 1)]

    def halo(value, sx, sz):
        def partner(i, j, k):
            return i if sx is None else mate(i, nx, sx), j, k if sz is None else mate(k, nz, sz)

        return exchange(value, counts, partner)

    halos = spread_out([halo(value, *seconds[i]) for i, value in zip(spots, packed)])

    parts = [sens, halos[0]] if deep else [sens, halos[0], halos[2], halos[4]]
    near = pl.pallas_call(
        join_kernel, out_shape=struct(len(parts) * size, cy), in_specs=[VM] * len(parts), out_specs=VM,
        compiler_params=PARAMS, name="join",
    )(*parts)
    far, reach = None, 2
    while reach < nx:
        if far is not None:
            near = jnp.concatenate([near, far])
        far = exchange(near, counts, lambda i, j, k, reach=reach: (i ^ reach, j, k))
        reach = 2 * reach

    depth = cz + 8
    y_face = struct(FIELDS // 3, depth, cy)

    def strip(own, *refs):
        count = len(spots)
        strip_kernel(own, *spread_out(refs[:count]), *refs[count:], dims=dims, counts=counts)

    ext, strips, ya, yb = pl.pallas_call(
        strip, out_shape=[pltpu.VMEM((FIELDS, planes * wide, cy), jnp.float32), struct(FIELDS, 2, depth, cy), y_face, y_face],
        in_specs=[VM] * (1 + len(spots)), out_specs=[VM] * 4,
        scratch_shapes=[pltpu.VMEM((FIELDS, 8 * cx, cy), jnp.float32), pltpu.VMEM((FIELDS, 2 * W, 8, cy), jnp.float32)],
        compiler_params=PARAMS, name="strip",
    )(fields, *[halos[i] for i in spots])

    second = ny - 1 if ny == 4 else ny
    joined = (1, second)
    line_rows = STEPS * short + 8
    strip_rows = FIELDS // 3 * depth

    def lines(*refs):
        if far is None:
            refs = refs[:1] + (None,) + refs[1:]
        lines_kernel(*refs, dims=dims, counts=counts, rows=rows, joined=joined)

    gathered = [near] if far is None else [near, far]
    forced = pl.pallas_call(
        lines, out_shape=[struct(line_rows + (strip_rows if k in joined else 0), cy) for k in range(ny)],
        in_specs=[VM] * (len(gathered) + 2), out_specs=[VM] * ny,
        scratch_shapes=[pltpu.VMEM((ny + 2, STEPS * short, cy), jnp.float32)], compiler_params=PARAMS, name="lines",
    )(*gathered, ya, yb)
    forced = [forced[0]] + [exchange(forced[k], counts, lambda i, j, m, k=k: (i, j ^ k, m)) for k in range(1, ny)]
    if second == ny:
        yb = exchange(yb, counts, lambda i, j, k: (i, mate(j, ny, 1), k))
    if deep:
        total = sum(f[f.shape[0] - line_rows:] for f in forced)
        total = lax.psum(total, "gz")
        forced = [total, jnp.concatenate([forced[1][:strip_rows], jnp.zeros_like(total)])] + (
            [jnp.concatenate([forced[3][:strip_rows], jnp.zeros_like(total)])] if second < ny else []
        )
        joined = (1, 2)
    if second == ny:
        joined = (1, len(forced))
        forced.append(jnp.concatenate([yb.reshape(strip_rows, cy), jnp.zeros((line_rows, cy), jnp.float32)]))

    def steps(*refs):
        steps_kernel(*refs, dims=dims, counts=counts, lines=len(forced), joined=joined)

    three = pltpu.VMEM((3, planes * short + 8, cy), jnp.float32)
    whole = pltpu.VMEM((planes * wide, cy), jnp.float32)
    out_v, out_p, out_s = pl.pallas_call(
        steps, out_shape=[struct(3, cz * cx, cy), struct(cz * cx, cy), struct(cz * cx, cy)],
        in_specs=[VM] * (2 + len(forced)), out_specs=[VM] * 3,
        scratch_shapes=[
            pltpu.VMEM((line_rows, cy), jnp.float32), whole, pltpu.VMEM((3, planes * wide, cy), jnp.float32),
            three, three, three, three, three,
        ],
        compiler_params=PARAMS, name="steps",
    )(ext, strips, *forced)
    return out_v.reshape(3, cz, cx, cy), out_p.reshape(cz, cx, cy), out_s.reshape(cz, cx, cy)


def solution(mesh):
    return jax.shard_map(
        shards,
        mesh=mesh,
        in_specs=(
            P(None, "gz", "gx", "gy"),
            P("gz", "gx", "gy"),
            P("gz", "gx", "gy"),
            P(None, "gz", "gx", "gy"),
            P("gz", "gx", "gy"),
            P(("gx", "gy", "gz"), None),
            P(("gx", "gy", "gz"), None),
            P(("gx", "gy", "gz")),
            P(("gx", "gy", "gz")),
        ),
        out_specs=(P(None, "gz", "gx", "gy"), P("gz", "gx", "gy"), P("gz", "gx", "gy")),
        check_vma=False,
    )
```

```python
import functools

import jax
import jax.numpy as jnp
from jax import lax
from jax.experimental import pallas as pl
from jax.experimental.pallas import tpu as pltpu
from jax.sharding import PartitionSpec as P

STEPS = 2
W = 2
COLS = 3 * W
FIELDS = 9
AXES = ("gx", "gy", "gz")


def mate(index, count, second):
    other = index + 1 if (index + second) % 2 == 0 else index - 1
    return other if 0 <= other < count else index


def exchange(value, shape, partner):
    nx, ny, nz = shape
    pairs = []
    for i in range(nx):
        for j in range(ny):
            for k in range(nz):
                a, b, c = partner(i, j, k)
                pairs.append(((i * ny + j) * nz + k, (a * ny + b) * nz + c))
    return lax.ppermute(value, AXES, pairs)


def even(index):
    return lax.rem(index, 2) == 0


VM = pl.BlockSpec(memory_space=pltpu.VMEM)
HBM = pl.BlockSpec(memory_space=pltpu.HBM)
PARAMS = pltpu.CompilerParams(vmem_limit_bytes=40 * 1024 * 1024)


def struct(*shape):
    return jax.ShapeDtypeStruct(shape, jnp.float32)


BASE = 8
EDGE_ROWS = 8 * -(-FIELDS * W * W // 8)


def rows_of(dims):
    cz, cx, _ = dims
    return cz + 2 * W + 1, cx + 2 * BASE, cx + 8


def pack_kernel(vel, pres, mod, av, ap, values, owner, line, step, fields, xa, xb, za, zb, xza, xzb, xzc, xzd, sens, *scratch, dims):
    cz, cx, cy = dims
    own, inputs, sem = scratch[0], scratch[1:4], scratch[4]
    rows = own.shape[0]
    ex, ez = even(lax.axis_index("gx")), even(lax.axis_index("gz"))
    copies = [
        (vel, fields.at[pl.ds(0, 3)]),
        (pres, fields.at[3]),
        (mod, fields.at[4]),
        (av, fields.at[pl.ds(5, 3)]),
        (ap, fields.at[8]),
        (values, own),
        (owner, inputs[0]),
        (line, inputs[1]),
        (step, inputs[2]),
    ]
    copies = [pltpu.make_async_copy(a, b, sem.at[i]) for i, (a, b) in enumerate(copies)]
    for copy in copies:
        copy.start()
    for copy in copies[5:]:
        copy.wait()
    first_row = [inputs[i][...] for i in range(3)]
    code = first_row[0] * (STEPS * cx) + first_row[2] * cx + first_row[1]
    sens[0:rows, :] = own[...]
    sens[rows:rows + 8, :] = jnp.zeros((8, cy), jnp.float32)
    sens[rows:rows + 1, 0:rows] = code.astype(jnp.float32)
    x_rows, z_rows = FIELDS * W * cz, FIELDS * W * cx
    for face, at in ((xa, x_rows), (za, z_rows), (xza, EDGE_ROWS)):
        face[at:at + rows + 8, :] = sens[...]
    for copy in copies[:5]:
        copy.wait()
    for f in range(FIELDS):
        for l in range(W):
            first = fields[f, pl.ds(l, cz, stride=cx), :]
            last = fields[f, pl.ds(cx - W + l, cz, stride=cx), :]
            a = jnp.where(ex, last, first)
            b = jnp.where(ex, first, last)
            xa[pl.ds((f * W + l) * cz, cz), :] = a
            xb[pl.ds((f * W + l) * cz, cz), :] = b
            for x, (near, far) in ((a, (xza, xzc)), (b, (xzb, xzd))):
                near[pl.ds((f * W + l) * W, W), :] = jnp.where(ez, x[cz - W:], x[:W])
                if far is not None:
                    far[pl.ds((f * W + l) * W, W), :] = jnp.where(ez, x[:W], x[cz - W:])
            low = fields[f, pl.ds(l * cx, cx), :]
            high = fields[f, pl.ds((cz - W + l) * cx, cx), :]
            za[pl.ds((f * W + l) * cx, cx), :] = jnp.where(ez, high, low)
            if zb is not None:
                zb[pl.ds((f * W + l) * cx, cx), :] = jnp.where(ez, low, high)


def join_kernel(*refs, count):
    ins, out = refs[:count], refs[-1]
    rows = out.shape[0] // count
    for i, ref in enumerate(ins):
        out[i * rows:(i + 1) * rows, :] = ref[ref.shape[0] - rows:, :]


def fill(ext, depths, edges, fields, xs, zs, xzs, dims, place):
    cz, cx, cy = dims
    _, wide, _ = rows_of(dims)
    (ix, nx), _, (iz, nz) = place
    ex, ez = even(ix), even(iz)
    has = {"xl": ix > 0, "xh": ix < nx - 1, "zl": iz > 0, "zh": iz < nz - 1}

    def sides(pair, parity, low, high):
        a, b = pair
        below = jnp.where(parity, 0.0 if b is None else b, a)
        above = jnp.where(parity, a, 0.0 if b is None else b)
        return jnp.where(low, below, 0.0), jnp.where(high, above, 0.0)

    for f in range(FIELDS):
        for plane in range(cz):
            ext[f, pl.ds((plane + W) * wide + BASE, cx), :] = fields[f, pl.ds(plane * cx, cx), :]
        depths[f, pl.ds(W * cx, (8 - 2 * W) * cx), :] = jnp.zeros(((8 - 2 * W) * cx, cy), jnp.float32)
        for l in range(W):
            n = f * W + l
            low, high = sides([x[pl.ds(n * cz, cz), :] for x in xs], ex, has["xl"], has["xh"])
            ext[f, pl.ds(W * wide + BASE + cx + l, cz, stride=wide), :] = high
            ext[f, pl.ds(W * wide + BASE - W + l, cz, stride=wide), :] = low
            low, high = sides([None if z is None else z[pl.ds(n * cx, cx), :] for z in zs], ez, has["zl"], has["zh"])
            ext[f, pl.ds(l * wide + BASE, cx), :] = low
            ext[f, pl.ds((cz + W + l) * wide + BASE, cx), :] = high
            depths[f, pl.ds((8 - W + l) * cx, cx), :] = low
            depths[f, pl.ds(l * cx, cx), :] = high
            got = [None if c is None else c[pl.ds(n * W, W), :] for c in xzs]
            near = sides(got[:2], ex, has["xl"], has["xh"])
            far = sides(got[2:], ex, has["xl"], has["xh"]) if got[2] is not None else (None, None)
            for part, row in ((0, BASE - W + l), (1, BASE + cx + l)):
                low, high = sides((near[part], far[part]), ez, has["zl"], has["zh"])
                edges[f, part * W + l] = jnp.concatenate([high, jnp.zeros((8 - 2 * W, cy), jnp.float32), low])
                for k in range(W):
                    ext[f, pl.ds(k * wide + row, 1), :] = low[k:k + 1]
                    ext[f, pl.ds((cz + W + k) * wide + row, 1), :] = high[k:k + 1]


def lane_of(shape):
    return lax.broadcasted_iota(jnp.int32, shape, 1)


def roll(value, by, axis):
    size = value.shape[axis]
    return pltpu.roll(value, by % size, axis)


def add_strips(low, high, row, x, cy, bounded=False):
    at = COLS * (x + W)
    lane = lane_of(row.shape)
    here, there = lane >= at + W, lane >= at
    if bounded:
        here, there = here & (lane < at + COLS), there & (lane < at + 2 * W)
    low = jnp.where(here, roll(row, at + W, 1), low)
    high = jnp.where(there, roll(row, at - (cy - 2 * W), 1), high)
    return low, high


def own_kernel(fields, strips, *, dims):
    cz, cx, cy = dims
    for f in range(FIELDS):
        low = jnp.zeros((cz, cy), jnp.float32)
        high = jnp.zeros((cz, cy), jnp.float32)
        for x in range(cx):
            low, high = add_strips(low, high, fields[f, pl.ds(x, cz, stride=cx), :], x, cy)
        strips[f, 0] = low
        strips[f, 1] = high


def halo_kernel(fields, mine, xa, xb, za, zb, xza, xzb, xzc, xzd, ext, strips, ya, yb, depths, edges, *, dims, counts):
    cz, cx, cy = dims
    _, wide, _ = rows_of(dims)
    planes = cz + 8
    place = [(lax.axis_index(a), n) for a, n in zip(AXES, counts)]
    fill(ext, depths, edges, fields, (xa, xb), (za, zb), (xza, xzb, xzc, xzd), dims, place)
    ey = even(place[1][0])
    lane = lane_of((planes, cy))
    middle = (lane % COLS >= W) & (lane % COLS < 2 * W)
    halo = list(range(-W, 0)) + list(range(cx, cx + W))
    for g in range(FIELDS // 3):
        outs = [jnp.zeros((planes, cy), jnp.float32)] * 2
        for j in range(3):
            f = 3 * g + j
            low, high = mine[f, 0], mine[f, 1]
            for x in halo:
                row = ext[f, pl.ds(W * wide + BASE + x, cz, stride=wide), :]
                low, high = add_strips(low, high, row, x, cy, True)
            below = jnp.zeros((8, cy), jnp.float32)
            above = jnp.zeros((8, cy), jnp.float32)
            for x in range(-W, cx + W):
                row = depths[f, pl.ds(x, 8, stride=cx), :] if 0 <= x < cx else edges[f, x + W if x < 0 else x - cx + W]
                below, above = add_strips(below, above, row, x, cy)
            low, high = jnp.concatenate([low, below]), jnp.concatenate([high, above])
            strips[f, 0] = low
            strips[f, 1] = high
            for n, (odd_side, even_side) in enumerate(((low, high), (high, low))):
                edge = jnp.where(middle, jnp.where(ey, even_side, odd_side), 0.0)
                outs[n] = outs[n] + roll(edge, W * (j - 1), 1)
        ya[g] = outs[0]
        yb[g] = outs[1]


def lines_kernel(own_rows, far_rows, ya, yb, before, *refs, dims, counts, rows, joined):
    _, cx, cy = dims
    nx, ny, _ = counts
    _, _, wide = rows_of(dims)
    outs, dense = refs[:ny], refs[ny]
    ix, iy = lax.axis_index("gx"), lax.axis_index("gy")
    size = rows + 8
    ins = [(ref, i * size) for ref in (own_rows, far_rows) if ref is not None for i in range(ref.shape[0] // size)]
    values = jnp.concatenate([r[at:at + rows, :] for r, at in ins], axis=0)
    code = jnp.concatenate([r[at + rows:at + rows + 1, 0:rows] for r, at in ins], axis=1).astype(jnp.int32)
    owner, rest = code // (STEPS * cx), code % (STEPS * cx)
    step, line = rest // cx, rest % cx
    ox, oy = owner // ny, owner % ny
    row = (ox - ix) * cx + line + W
    key = jnp.where((row >= 0) & (row < cx + 2 * W), (oy * STEPS + step) * wide + row, -1)
    table = lax.broadcasted_iota(jnp.int32, (ny * STEPS * wide, len(ins) * rows), 0) == key
    spread = jnp.dot(
        table.astype(jnp.float32), values, precision=lax.Precision.HIGHEST, preferred_element_type=jnp.float32
    )
    block = STEPS * wide
    dense[0] = jnp.zeros((block, cy), jnp.float32)
    dense[ny + 1] = jnp.zeros((block, cy), jnp.float32)
    for b in range(ny):
        dense[b + 1] = spread[b * block:(b + 1) * block]
    lane = lane_of((1, cy))
    for k in range(ny):
        out, base = outs[k], 0
        if k in joined:
            strip = (ya, yb)[joined.index(k)]
            base = strip.shape[0] * strip.shape[1]
            out[0:base, :] = strip[...].reshape(base, cy)
        at = lax.bitwise_xor(iy, k)
        own, below, above = dense[at + 1], dense[at], dense[at + 2]
        out[base:base + block, :] = own
        out[base + block:base + block + 8, :] = jnp.zeros((8, cy), jnp.float32)
        for s in range(STEPS):
            low = jnp.zeros((1, cy), jnp.float32)
            high = jnp.zeros((1, cy), jnp.float32)
            for x in range(-W, cx + W):
                r = s * wide + x + W
                start = COLS * (x + W)
                low = jnp.where(lane >= start, roll(below[r:r + 1], start - (cy - W), 1), low)
                low, high = add_strips(low, high, own[r:r + 1], x, cy)
                high = jnp.where(lane >= start + 2 * W, roll(above[r:r + 1], start + 2 * W, 1), high)
            out[base + block + 2 * s:base + block + 2 * s + 1, :] = low
            out[base + block + 2 * s + 1:base + block + 2 * s + 2, :] = high


def strip_steps(s, mask, f1, f0):
    v, p, mod, av, ap = s[0:3], s[3], s[4], s[5:8], s[8]

    def keep(a):
        return jnp.where(mask, a, 0.0)

    def lap(a):
        total = roll(a, 1, 0) + roll(a, -1, 0) + roll(a, COLS, 1) + roll(a, -COLS, 1) + roll(a, 1, 1) + roll(a, -1, 1)
        return total - 6.0 * a

    def div(u):
        return (u[0] - roll(u[0], COLS, 1)) + (u[1] - roll(u[1], 1, 1)) + (u[2] - roll(u[2], 1, 0))

    def grad(q):
        return roll(q, -COLS, 1) - q, roll(q, -1, 1) - q, roll(q, -1, 0) - q

    b0 = [lap(a) for a in v]
    g = grad(keep(p + div(v)))
    v1 = [keep(v[c] + 0.25 * (g[c] + mod * b0[c])) for c in range(3)]
    av = [av[0], av[1], av[2] + f1]
    shear = sum(av[c] * lap(v1[c]) for c in range(3))
    m = keep(ap - 0.25 * div(av))
    g = grad(m)
    av = [keep(av[c] + 0.25 * lap(mod * av[c]) - g[c]) for c in range(3)]
    av = [av[0], av[1], av[2] + f0]
    shear = 0.25 * (shear + sum(av[c] * b0[c] for c in range(3)))
    m = keep(m - 0.25 * div(av))
    g = grad(m)
    av = [av[c] + 0.25 * lap(mod * av[c]) - g[c] for c in range(3)]
    return av + [m, shear]


def lap(below, a, above, lower, upper):
    return (above + below) + (lower + upper) + (roll(a, 1, 1) + roll(a, -1, 1)) - 6.0 * a


def first_kernel(ext, b0, v1, a1, w1, m0, w0, *, dims, counts):
    cz, cx, cy = dims
    _, wide, short = rows_of(dims)
    (ix, nx), _, (iz, nz) = [(lax.axis_index(a), n) for a, n in zip(AXES, counts)]

    row = lax.broadcasted_iota(jnp.int32, (short, cy), 0)
    inside1 = ((row > 0) & (row <= cx)) | ((row > cx) & (ix < nx - 1)) | ((row == 0) & (ix > 0))

    def keep(a, plane):
        at = iz * cz + plane - W
        return jnp.where(inside1 & ((at >= 0) & (at < nz * cz)), a, 0.0)

    def wider(f, plane, dx=0):
        return ext[f, pl.ds(plane * wide + (BASE - 1 + dx), short), :]

    def weight(c, plane, dx=0):
        return w0[c, pl.ds(plane * wide + (BASE - 1 + dx), short), :]

    def weigh(plane, _):
        at = pl.ds(pl.multiple_of(plane * wide, 8), wide)
        for c in range(3):
            w0[c, at, :] = ext[4, at, :] * ext[5 + c, at, :]
        return 0

    def pressure(plane, base, q, scale):
        vx, vy, vz = (wider(base + c, plane) for c in range(3))
        d = (vx - wider(base, plane, -1)) + (vy - roll(vy, 1, 1)) + (vz - wider(base + 2, plane - 1))
        return keep(wider(q, plane) + scale * d, plane)

    def whole(plane):
        return pl.ds(pl.multiple_of(plane * short, 8), short)

    def first(plane, carry):
        p1, m = carry
        p1_above = pressure(plane + 1, 0, 3, 1.0)
        m_above = pressure(plane + 1, 5, 8, -0.25)
        m0[whole(plane + 1), :] = m_above
        g = (roll(p1, -1, 0) - p1, roll(p1, -1, 1) - p1, p1_above - p1)
        h = (roll(m, -1, 0) - m, roll(m, -1, 1) - m, m_above - m)
        mod = wider(4, plane)
        for c in range(3):
            v = wider(c, plane)
            bend = lap(wider(c, plane - 1), v, wider(c, plane + 1), wider(c, plane, -1), wider(c, plane, 1))
            b0[c, whole(plane), :] = bend
            v1[c, whole(plane), :] = keep(v + 0.25 * (g[c] + mod * bend), plane)
            a = wider(5 + c, plane)
            spring = lap(weight(c, plane - 1), weight(c, plane), weight(c, plane + 1), weight(c, plane, -1), weight(c, plane, 1))
            a = keep(a + 0.25 * spring - h[c], plane)
            a1[c, whole(plane), :] = a
            w1[c, whole(plane), :] = mod * a
        return p1_above, m_above

    lax.fori_loop(0, cz + 2 * W, weigh, 0, unroll=4)
    begin = (pressure(1, 0, 3, 1.0), pressure(1, 5, 8, -0.25))
    m0[whole(1), :] = begin[1]
    lax.fori_loop(1, cz + W + 1, first, begin, unroll=2)


def second_kernel(ext, b0, v1, a1, w1, m0, out_v, out_p, out_s, bends, *, dims, counts):
    cz, cx, cy = dims
    _, wide, short = rows_of(dims)
    (ix, nx), _, (iz, nz) = [(lax.axis_index(a), n) for a, n in zip(AXES, counts)]

    row = lax.broadcasted_iota(jnp.int32, (short, cy), 0)
    inside0 = (row < cx) | (ix < nx - 1)

    def keep(a, plane):
        at = iz * cz + plane - W
        return jnp.where(inside0 & ((at >= 0) & (at < nz * cz)), a, 0.0)

    def step(ref, c, plane, dx=0, count=cx):
        return ref[c, pl.ds(plane * short + (1 + dx), count), :]

    def pressure1(plane):
        ax, ay, az = (step(a1, c, plane, 0, short) for c in range(3))
        d = (ax - step(a1, 0, plane, -1, short)) + (ay - roll(ay, 1, 1)) + (az - step(a1, 2, plane - 1, 0, short))
        return keep(m0[pl.ds(plane * short + 1, short), :] - 0.25 * d, plane)

    def second(plane, m):
        m_above = pressure1(plane + 1)
        upper = roll(m, -1, 0)[:cx]
        m, above = m[:cx], m_above[:cx]
        h = (upper - m, roll(m, -1, 1) - m, above - m)
        own = pl.ds(pl.multiple_of((plane - W) * cx, 8), cx)
        shear = jnp.zeros((cx, cy), jnp.float32)
        for c in range(3):
            a = step(a1, c, plane)
            bend = lap(
                step(v1, c, plane - 1), step(v1, c, plane), step(v1, c, plane + 1), step(v1, c, plane, -1),
                step(v1, c, plane, 1),
            )
            spring = lap(
                step(w1, c, plane - 1), step(w1, c, plane), step(w1, c, plane + 1), step(w1, c, plane, -1),
                step(w1, c, plane, 1),
            )
            at_first = ext[5 + c, pl.ds(pl.multiple_of(plane * wide + BASE, 8), cx), :]
            shear = shear + (at_first * bend + a * step(b0, c, plane))
            out_v[c, own, :] = a + 0.25 * spring - h[c]
        out_p[own, :] = m
        out_s[own, :] = 0.25 * shear
        return m_above

    lax.fori_loop(W, cz + W, second, pressure1(W), unroll=2)
    for c in range(3):
        for k in range(2):
            bends[3 * k + c] = step(b0, c, W + k)
    bends[6] = lap(
        step(v1, 2, W - 1), step(v1, 2, W), step(v1, 2, W + 1), step(v1, 2, W, -1), step(v1, 2, W, 1)
    )


def forcing_steps(force, ext, bends, dims, place):
    cz, cx, cy = dims
    _, wide, short = rows_of(dims)
    ix, nx = place[0]
    f0, f1 = force[0:short, :], force[pl.ds(short, short), :]
    mod = [ext[4, pl.ds((W + z) * wide + BASE - W, short), :] for z in range(2)]
    x = lax.broadcasted_iota(jnp.int32, (short, cy), 0) - W
    inside = ((x >= 0) & (x < cx)) | ((x >= cx) & (ix < nx - 1)) | ((x < 0) & (ix > 0))

    def keep(a):
        return jnp.where(inside, a, 0.0)

    def flat(a):
        return roll(a, 1, 0) + roll(a, -1, 0) + roll(a, 1, 1) + roll(a, -1, 1) - 6.0 * a

    def grad(q):
        return [roll(q, -1, 0) - q, roll(q, -1, 1) - q]

    w = mod[0] * f1
    m = [-0.25 * f1, 0.25 * f1]
    g = [grad(q) for q in m]
    a = [
        [keep(-g[0][0]), keep(-g[0][1]), keep(f1 + 0.25 * flat(w) - (m[1] - m[0])) + f0],
        [keep(-g[1][0]), keep(-g[1][1]), keep(0.25 * w + m[1])],
    ]
    w = [[mod[z] * a[z][c] for c in range(3)] for z in range(2)]

    def div(u):
        return (u[0] - roll(u[0], 1, 0)) + (u[1] - roll(u[1], 1, 1)) + u[2]

    m = [keep(m[0] - 0.25 * div(a[0])), keep(m[1] - 0.25 * (div(a[1]) - a[0][2])), keep(0.25 * a[1][2])]
    g = [grad(q) for q in m]
    deep = [m[1] - m[0], m[2] - m[1], -m[2]]
    own = slice(W, W + cx)
    out = []
    for z in range(3):
        add = []
        for c in range(3):
            spring = (flat(w[z][c]) + w[1 - z][c]) if z < 2 else w[1][c]
            start = a[z][c] if z < 2 else 0.0
            add.append((start + 0.25 * spring - (g[z][c] if c < 2 else deep[z]))[own])
        add.append(m[z][own])
        if z < 2:
            meet = sum(a[z][c][own] * bends[3 * z + c] for c in range(3))
            add.append(0.25 * (meet + f1[own] * bends[6] if z == 0 else meet))
        out.append(add)
    return out


def finish_kernel(ext, strips, main_v, main_p, main_s, bends, *rest, dims, counts, lines, joined):
    cz, cx, cy = dims
    _, wide, short = rows_of(dims)
    planes = cz + 8
    forced = rest[:lines]
    out_v, out_p, out_s, force, stage, sem = rest[lines:]
    place = [(lax.axis_index(a), n) for a, n in zip(AXES, counts)]
    (ix, nx), (iy, ny), (iz, nz) = place
    block = STEPS * short
    size = block + 8
    total = forced[0][forced[0].shape[0] - size:, :]
    for ref in forced[1:]:
        total = total + ref[ref.shape[0] - size:, :]
    force[...] = jnp.where(iz == 0, total, 0.0)

    lane = lane_of((planes, cy))
    depth = lax.broadcasted_iota(jnp.int32, (planes, cy), 0)
    x, col = lane // COLS - W, lane % COLS
    z = jnp.where(depth < cz + W, depth, depth - planes)
    gx, gz = ix * cx + x, iz * cz + z
    solid = (x < cx + W) & (gx >= 0) & (gx < nx * cx) & (gz >= 0) & (gz < nz * cz)
    ey = even(iy)
    yfrom = [forced[k] for k in joined]
    results = []
    for side in range(2):
        s = []
        for f in range(FIELDS):
            g, j = f // 3, f % 3
            a, b = (ref[pl.ds(g * planes, planes), :] for ref in yfrom)
            if side == 0:
                fresh = jnp.where(iy > 0, roll(jnp.where(ey, b, a), -W * j, 1), 0.0)
                s.append(jnp.where(col < W, fresh, strips[f, 0]))
            else:
                fresh = jnp.where(iy < ny - 1, roll(jnp.where(ey, a, b), 2 * W - W * j, 1), 0.0)
                s.append(jnp.where(col >= 2 * W, fresh, strips[f, 1]))
        beyond = (col >= W) | (iy > 0) if side == 0 else (col < 2 * W) | (iy < ny - 1)
        top = depth == 0
        push = [jnp.where(top, force[pl.ds(block + 2 * t + side, 1), :], 0.0) for t in range(STEPS)]
        results.append(strip_steps(s, solid & beyond, push[1], push[0]))
    added = forcing_steps(force, ext, bends, dims, place)
    mains = [main_v.at[0], main_v.at[1], main_v.at[2], main_p, main_s]
    outs = [out_v.at[0], out_v.at[1], out_v.at[2], out_p, out_s]
    lane = lane_of((cz, cy))
    copies = []
    for n, (low, high, main, out) in enumerate(zip(*results, mains, outs)):
        reach = [add[n] for add in added if n < len(add)]
        done = len(reach) * cx
        stage[n, 0:done, :] = main[0:done, :] + jnp.concatenate(reach)
        stage[n, done:, :] = main[done:, :]
        low, high = low[:cz], high[:cz]
        for x0 in range(cx):
            start = COLS * (x0 + W)
            value = stage[n, pl.ds(x0, cz, stride=cx), :]
            value = jnp.where(lane < W, roll(low, -(start + W), 1), value)
            value = jnp.where(lane >= cy - W, roll(high, cy - W - (start + W), 1), value)
            stage[n, pl.ds(x0, cz, stride=cx), :] = value
        copy = pltpu.make_async_copy(stage.at[n], out, sem.at[n])
        copy.start()
        copies.append(copy)
    for copy in copies:
        copy.wait()


def shards(vel, pres, modulus, adj_vel_in, adj_pres_in, sensor_values, sensor_owner, sensor_line, sensor_step):
    counts = tuple(lax.axis_size(a) for a in AXES)
    nx, ny, nz = counts
    dims = pres.shape
    cz, cx, cy = dims
    rows = sensor_values.shape[0]
    size = rows + 8
    planes, wide, short = rows_of(dims)
    deep = nz > 2

    x_rows, z_rows, edge_rows = FIELDS * W * cz, FIELDS * W * cx, EDGE_ROWS
    faces = [x_rows + size, x_rows, z_rows + size, z_rows if deep else None]
    faces += [edge_rows + size, edge_rows, edge_rows if deep else None, edge_rows if deep else None]
    spots = [i for i, n in enumerate(faces) if n is not None]

    def spread_out(refs):
        full = [None] * 8
        for i, ref in zip(spots, refs):
            full[i] = ref
        return full

    def pack(*refs):
        count = 10 + len(spots)
        pack_kernel(*refs[:10], *spread_out(refs[10:count]), *refs[count:], dims=dims)

    small = pltpu.VMEM((1, rows), jnp.int32)
    inputs = [
        vel.reshape(3, cz * cx, cy), pres.reshape(cz * cx, cy), modulus.reshape(cz * cx, cy),
        adj_vel_in.reshape(3, cz * cx, cy), adj_pres_in.reshape(cz * cx, cy), sensor_values,
        sensor_owner.reshape(1, rows), sensor_line.reshape(1, rows), sensor_step.reshape(1, rows),
    ]
    fields, *packed, sens = pl.pallas_call(
        pack, out_shape=[pltpu.VMEM((FIELDS, cz * cx, cy), jnp.float32)] + [struct(faces[i], cy) for i in spots] + [struct(size, cy)],
        in_specs=[HBM] * 9, out_specs=[VM] * (len(spots) + 2),
        scratch_shapes=[pltpu.VMEM((rows, cy), jnp.float32), small, small, small, pltpu.SemaphoreType.DMA((9,))],
        compiler_params=PARAMS, name="pack",
    )(*[pltpu.with_memory_space_constraint(x, pltpu.HBM) for x in inputs])
    seconds = [(0, None), (1, None), (None, 0), (None, 1), (0, 0), (1, 0), (0, 1), (1, 1)]

    def halo(value, sx, sz):
        def partner(i, j, k):
            a, c = i if sx is None else mate(i, nx, sx), k if sz is None else mate(k, nz, sz)
            return (a, j, c) if (a, c) != (i, k) else (a, mate(j, ny, 0), c)

        return exchange(value, counts, partner)

    halos = spread_out([halo(value, *seconds[i]) for i, value in zip(spots, packed)])

    mine = pl.pallas_call(
        functools.partial(own_kernel, dims=dims), out_shape=struct(FIELDS, 2, cz, cy), in_specs=[VM], out_specs=VM,
        compiler_params=PARAMS, name="own",
        cost_estimate=pl.CostEstimate(flops=20_000_000, bytes_accessed=4_000_000, transcendentals=0),
    )(fields)

    parts = [sens, halos[0]] if deep else [sens, halos[0], halos[2], halos[4]]
    rest = [x for x in halos if x is not None and not any(x is p for p in parts)] + [mine]
    near = pl.pallas_call(
        functools.partial(join_kernel, count=len(parts)), out_shape=struct(len(parts) * size, cy),
        in_specs=[VM] * len(parts + rest), out_specs=VM, compiler_params=PARAMS, name="join",
    )(*parts, *rest)
    far, reach = None, 2
    while reach < nx:
        if far is not None:
            near = jnp.concatenate([near, far])
        far = exchange(near, counts, lambda i, j, k, reach=reach: (i ^ reach, j, k))
        reach = 2 * reach

    depth = cz + 8
    y_face = struct(FIELDS // 3, depth, cy)

    def halo_fill(own, strips, *refs):
        count = len(spots)
        halo_kernel(own, strips, *spread_out(refs[:count]), *refs[count:], dims=dims, counts=counts)

    ext, strips, ya, yb = pl.pallas_call(
        halo_fill, out_shape=[pltpu.VMEM((FIELDS, planes * wide, cy), jnp.float32), struct(FIELDS, 2, depth, cy), y_face, y_face],
        in_specs=[VM] * (2 + len(spots)), out_specs=[VM] * 4,
        scratch_shapes=[pltpu.VMEM((FIELDS, 8 * cx, cy), jnp.float32), pltpu.VMEM((FIELDS, 2 * W, 8, cy), jnp.float32)],
        compiler_params=PARAMS, name="halo",
    )(fields, mine, *[halos[i] for i in spots])

    three = pltpu.VMEM((3, planes * short + 8, cy), jnp.float32)
    middle = pl.pallas_call(
        functools.partial(first_kernel, dims=dims, counts=counts), out_shape=[three] * 4 + [pltpu.VMEM(three.shape[1:], jnp.float32)],
        in_specs=[VM], out_specs=[VM] * 5, scratch_shapes=[pltpu.VMEM((3, planes * wide, cy), jnp.float32)],
        compiler_params=PARAMS, name="first",
        cost_estimate=pl.CostEstimate(flops=30_000_000, bytes_accessed=10_000_000, transcendentals=0),
    )(ext)

    second = ny - 1 if ny == 4 else ny
    joined = (1, second)
    line_rows = STEPS * short + 8
    strip_rows = FIELDS // 3 * depth

    def lines(*refs):
        if far is None:
            refs = refs[:1] + (None,) + refs[1:]
        lines_kernel(*refs, dims=dims, counts=counts, rows=rows, joined=joined)

    gathered = [near] if far is None else [near, far]
    forced = pl.pallas_call(
        lines, out_shape=[struct(line_rows + (strip_rows if k in joined else 0), cy) for k in range(ny)],
        in_specs=[VM] * (len(gathered) + 3), out_specs=[VM] * ny,
        scratch_shapes=[pltpu.VMEM((ny + 2, STEPS * short, cy), jnp.float32)], compiler_params=PARAMS, name="lines",
    )(*gathered, ya, yb, middle[-1])
    forced = [forced[0]] + [exchange(forced[k], counts, lambda i, j, m, k=k: (i, j ^ k, m)) for k in range(1, ny)]
    if second == ny:
        yb = exchange(yb, counts, lambda i, j, k: (i, mate(j, ny, 1), k))
    if deep:
        total = sum(f[f.shape[0] - line_rows:] for f in forced)
        total = lax.psum(total, "gz")
        forced = [total, jnp.concatenate([forced[1][:strip_rows], jnp.zeros_like(total)])] + (
            [jnp.concatenate([forced[3][:strip_rows], jnp.zeros_like(total)])] if second < ny else []
        )
        joined = (1, 2)
    if second == ny:
        joined = (1, len(forced))
        forced.append(jnp.concatenate([yb.reshape(strip_rows, cy), jnp.zeros((line_rows, cy), jnp.float32)]))

    one, triple = (cz * cx, cy), (3, cz * cx, cy)
    mains = pl.pallas_call(
        functools.partial(second_kernel, dims=dims, counts=counts),
        out_shape=[pltpu.VMEM(triple, jnp.float32), pltpu.VMEM(one, jnp.float32), pltpu.VMEM(one, jnp.float32), struct(7, cx, cy)],
        in_specs=[VM] * 6, out_specs=[VM] * 4,
        compiler_params=PARAMS, name="second",
        cost_estimate=pl.CostEstimate(flops=30_000_000, bytes_accessed=10_000_000, transcendentals=0),
    )(ext, *middle)

    def finish(*refs):
        finish_kernel(*refs, dims=dims, counts=counts, lines=len(forced), joined=joined)

    out_v, out_p, out_s = pl.pallas_call(
        finish, out_shape=[struct(*triple), struct(*one), struct(*one)],
        in_specs=[VM] * (6 + len(forced)), out_specs=[HBM] * 3,
        scratch_shapes=[
            pltpu.VMEM((line_rows, cy), jnp.float32), pltpu.VMEM((5,) + one, jnp.float32), pltpu.SemaphoreType.DMA((5,)),
        ],
        compiler_params=PARAMS, name="finish",
    )(ext, strips, *mains, *forced)
    return out_v.reshape(3, cz, cx, cy), out_p.reshape(cz, cx, cy), out_s.reshape(cz, cx, cy)


def solution(mesh):
    return jax.shard_map(
        shards,
        mesh=mesh,
        in_specs=(
            P(None, "gz", "gx", "gy"),
            P("gz", "gx", "gy"),
            P("gz", "gx", "gy"),
            P(None, "gz", "gx", "gy"),
            P("gz", "gx", "gy"),
            P(("gx", "gy", "gz"), None),
            P(("gx", "gy", "gz"), None),
            P(("gx", "gy", "gz")),
            P(("gx", "gy", "gz")),
        ),
        out_specs=(P(None, "gz", "gx", "gy"), P("gz", "gx", "gy"), P("gz", "gx", "gy")),
        check_vma=False,
    )
```
